32 devices in a mesh: sa: 4 (over y, x), sb: 2 (over core), sc: 4 (over z).
Axes of the slice: x: 2, y: 2, z: 4, core: 2. Of those that a mesh axis runs over, the one named last changes fastest.
Arguments:
- queries: float32 [16384, 2048], P(('sa', 'sb', 'sc')), may hold values from -6 to 6
- key_rows: float32 [16384, 2048], P(('sa', 'sb', 'sc')), may hold values from -6 to 6
- value_rows: float32 [16384, 2048], P(('sa', 'sb', 'sc')), may hold values from -6 to 6
- out_grad: float32 [16384, 2048], P(('sa', 'sb', 'sc')), may hold values from -6 to 6
- prefix_state: float32 [16, 128, 128], replicated, may hold values from -768 to 768
- suffix_state: float32 [16, 128, 128], replicated, may hold values from -768 to 768
Outputs:
- query_grad: bfloat16 [16384, 2048], P(('sa', 'sb', 'sc'))
- key_grad: bfloat16 [16384, 2048], P(('sa', 'sb', 'sc'))
- value_grad: bfloat16 [16384, 2048], P(('sa', 'sb', 'sc'))
The draws below stay inside these ranges and needn't reach their ends.
All inputs are finite; a program needn't handle non-finite values.
Results may differ from the reference program's by a relative error of at most 0.0019.
Values sent between devices are 32-bit elements; how exact they have to be, the bound alone decides.
No kernel may reach another device: no remote copies, remote signals or barrier semaphores. Data moves between devices by JAX's collectives and lax.ppermute only.
A program may use at most 576 MiB of HBM per device.

```python
import math
import jax
import jax.numpy as jnp
from jax import lax

H = 16
E = 128
TOK_DEV = 512
TOKENS = 16384


def shard_levels(stream_key, shape, cuts, least, top_value):
    level, own = 1.0, jax.random.fold_in(stream_key, 6)
    for dim, blocks in cuts:
        steps = jnp.exp(jax.random.uniform(jax.random.fold_in(own, dim), (blocks,), jnp.float32, least / len(cuts), top_value / len(cuts)))
        level = level * jnp.repeat(steps, shape[dim] // blocks).reshape([-1 if axis == dim else 1 for axis in range(len(shape))])
    return level


def gaussian(own_key, shape, scale, reach, cuts=(), kind=jnp.bfloat16):
    entries = jax.random.normal(own_key, shape, jnp.float32) * scale
    if len(cuts) > 0:
        entries = shard_levels(own_key, shape, cuts, -0.22, 0.18) * entries
    return jnp.clip(entries, min=-reach, max=reach).astype(kind)


def setup_inputs(seed: int = 0) -> dict:
    key_list = jax.random.split(jax.random.key(seed), 7)
    queries = gaussian(key_list[0], (TOKENS, H * E), 1.0, 6.0, ((0, 32),), jnp.float32)
    key_rows = gaussian(key_list[1], (TOKENS, H * E), 1.0, 6.0, ((0, 32),), jnp.float32)
    value_rows = gaussian(key_list[2], (TOKENS, H * E), 1.0, 6.0, ((0, 32),), jnp.float32)
    out_grad = gaussian(key_list[3], (TOKENS, H * E), 1.0, 6.0, ((0, 32),), jnp.float32)
    prefix_state = gaussian(key_list[4], (H, E, E), (TOKENS ** 0.5), 768.0, (), jnp.float32)
    suffix_state = gaussian(key_list[5], (H, E, E), (TOKENS ** 0.5), 768.0, (), jnp.float32)
    return dict(queries=queries, key_rows=key_rows, value_rows=value_rows, out_grad=out_grad, prefix_state=prefix_state, suffix_state=suffix_state)


def block_grads(query_t, key_t, value_t, grad_t, state_before, state_after, factor):
    count = query_t.shape[0]
    highest = lax.Precision.HIGHEST
    lower = (lax.broadcasted_iota(jnp.int32, (count, count), 0) >= lax.broadcasted_iota(jnp.int32, (count, count), 1)).astype(query_t.dtype)
    grad_scores = jnp.einsum('the,she->hts', grad_t, value_t, precision=highest) * lower
    attn_scores = jnp.einsum('thd,shd->hts', query_t, key_t, precision=highest) * lower
    query_grad = factor * (jnp.einsum('the,hde->thd', grad_t, state_before, precision=highest) + jnp.einsum('hts,shd->thd', grad_scores, key_t, precision=highest))
    key_grad = factor * (jnp.einsum('she,hed->shd', value_t, state_after, precision=highest) + jnp.einsum('hts,thd->shd', grad_scores, query_t, precision=highest))
    value_grad = factor * (jnp.einsum('shd,hed->she', key_t, state_after, precision=highest) + jnp.einsum('hts,the->she', attn_scores, grad_t, precision=highest))
    return (query_grad.astype(jnp.bfloat16), key_grad.astype(jnp.bfloat16), value_grad.astype(jnp.bfloat16))

def reference(queries, key_rows, value_rows, out_grad, prefix_state, suffix_state):
    block_count = TOKENS // TOK_DEV
    shaped = (block_count, TOK_DEV, H, E)
    query_blocks = queries.reshape(shaped)
    key_blocks = key_rows.reshape(shaped)
    value_blocks = value_rows.reshape(shaped)
    grad_blocks = out_grad.reshape(shaped)
    highest = lax.Precision.HIGHEST
    factor = 1.0 / math.sqrt(E * TOKENS)

    def local_terms(pieces):
        key_t, value_t, grad_t, query_t = pieces
        return (jnp.einsum('thd,the->hde', key_t, value_t, precision=highest), jnp.einsum('the,thd->hed', grad_t, query_t, precision=highest))
    kv_all, grad_all = lax.map(local_terms, (key_blocks, value_blocks, grad_blocks, query_blocks))

    def carry_step(carry, term):
        return (carry + term, carry)
    final_forward, before_all = lax.scan(carry_step, prefix_state, kv_all)
    final_backward, after_all = lax.scan(carry_step, suffix_state, grad_all, reverse=True)

    def one_block(pieces):
        query_t, key_t, value_t, grad_t, state_before, state_after = pieces
        return block_grads(query_t, key_t, value_t, grad_t, state_before, state_after, factor)
    query_grad, key_grad, value_grad = lax.map(one_block, (query_blocks, key_blocks, value_blocks, grad_blocks, before_all, after_all))
    return (query_grad.reshape(TOKENS, H * E), key_grad.reshape(TOKENS, H * E), value_grad.reshape(TOKENS, H * E))
```

```python
import functools
import math

import jax
import jax.numpy as jnp
from jax import lax
from jax.experimental import pallas as pl
from jax.experimental.pallas import tpu as pltpu
from jax.sharding import PartitionSpec as P

AXES = ("sa", "sb", "sc")
CUTS = ((4, False), (8, False), (4, True))
VMEM = 56 * 2**20
NN = (((1,), (0,)), ((), ()))
TN = (((0,), (0,)), ((), ()))


def split(x):
    high = x.astype(jnp.bfloat16)
    low = (x - high.astype(jnp.float32)).astype(jnp.bfloat16)
    return high, low


def wide(x):
    return jnp.concatenate(split(x), axis=1)


def fold(x):
    half = x.shape[1] // 2
    return x[:, :half] + x[:, half:]


def stacked(x):
    return jnp.concatenate([x, x], axis=0)


def dot(a, b):
    return lax.dot_general(a, b, NN, preferred_element_type=jnp.float32)


def outer(a, b):
    half = a.shape[1]
    full = fold(lax.dot_general(wide(a), wide(b), TN, preferred_element_type=jnp.float32))
    return full[:half] + full[half:]


def local_kernel(place_ref, q_ref, k_ref, v_ref, g_ref, out_ref):
    size = out_ref.shape[-1]
    for j in range(out_ref.shape[1]):
        columns = slice(j * size, (j + 1) * size)
        out_ref[0, j] = outer(k_ref[:, columns], v_ref[:, columns])
        out_ref[1, j] = outer(g_ref[:, columns], q_ref[:, columns])


def local_terms(first, count, arrays, size):
    rows = arrays[0].shape[0]
    step = 2 - count % 2
    place = (first // step).reshape(1).astype(jnp.int32)
    spec = pl.BlockSpec((rows, step * size), lambda i, place: (0, place[0] + i))
    return pl.pallas_call(
        local_kernel,
        grid_spec=pltpu.PrefetchScalarGridSpec(
            num_scalar_prefetch=1,
            grid=(count // step,),
            in_specs=[spec] * 4,
            out_specs=pl.BlockSpec((2, step, size, size), lambda i, place: (0, i, 0, 0)),
        ),
        out_shape=jax.ShapeDtypeStruct((2, count, size, size), jnp.float32),
        compiler_params=pltpu.CompilerParams(vmem_limit_bytes=VMEM),
        cost_estimate=pl.CostEstimate(
            flops=16 * count * rows * size * size, bytes_accessed=16 * count * rows * size, transcendentals=0
        ),
        name="local_terms",
    )(place, *arrays)


def head_grads(q, k, v, g, before, after):
    count, size = len(q), q[0].shape[1]
    row = lax.broadcasted_iota(jnp.int32, (size, size), 0)
    column = lax.broadcasted_iota(jnp.int32, (size, size), 1)
    lower, upper = row >= column, row <= column

    q_t, v_t, g_t = ([wide(x.T) for x in xs] for xs in (q, v, g))
    q, k, v, g = ([wide(x) for x in xs] for xs in (q, k, v, g))
    q_rows, k_rows, g_rows = ([stacked(x) for x in xs] for xs in (q, k, g))

    before_t, after, after_t = [before.T], [after], [after.T]
    for i in range(count - 1):
        j = count - 1 - i
        before_t.append(before_t[-1] + fold(dot(v_t[i], k_rows[i])))
        after.append(after[-1] + fold(dot(g_t[j], q_rows[j])))
        after_t.append(after[-1].T)
    after, after_t = after[::-1], after_t[::-1]

    def scores(a, b_t, mask):
        return wide(jnp.where(mask, fold(dot(a, stacked(b_t))), 0.0))

    def both(rows, state, weights, other_rows):
        left = jnp.concatenate([rows, weights], axis=1)
        right = jnp.concatenate([stacked(wide(state)), other_rows], axis=0)
        return fold(dot(left, right))

    for i in range(count):
        yield (
            both(g[i], before_t[i], scores(g[i], v_t[i], lower), k_rows[i]),
            both(v[i], after[i], scores(v[i], g_t[i], upper), q_rows[i]),
            both(k[i], after_t[i], scores(k[i], q_t[i], upper), g_rows[i]),
        )


def grads_kernel(factor, place_ref, q_ref, k_ref, v_ref, g_ref, state_ref, *rest):
    outs = rest[-3:]
    size = state_ref.shape[-1]
    for j in range(state_ref.shape[1]):
        columns = slice(j * size, (j + 1) * size)
        blocks = [
            [ref[i : i + size, columns] for i in range(0, q_ref.shape[0], size)]
            for ref in (q_ref, k_ref, v_ref, g_ref)
        ]
        for i, results in enumerate(head_grads(*blocks, state_ref[0, j], state_ref[1, j])):
            for ref, x in zip(outs, results):
                ref[i * size : (i + 1) * size, columns] = (factor * x).astype(ref.dtype)


def grads(first, arrays, state, outs, factor):
    rows, columns = arrays[0].shape
    count, size = state.shape[1], state.shape[2]
    step = 2 - count % 2
    place = (first // step).reshape(1).astype(jnp.int32)
    spec = pl.BlockSpec((rows, step * size), lambda i, place: (0, place[0] + i))
    state_spec = pl.BlockSpec((2, step, size, size), lambda i, place: (0, i, 0, 0))
    given = [] if outs is None else list(outs)
    return pl.pallas_call(
        functools.partial(grads_kernel, factor),
        grid_spec=pltpu.PrefetchScalarGridSpec(
            num_scalar_prefetch=1,
            grid=(count // step,),
            in_specs=[spec] * 4 + [state_spec] + [pl.BlockSpec(memory_space=pl.ANY)] * len(given),
            out_specs=[spec] * 3,
        ),
        out_shape=[jax.ShapeDtypeStruct((rows, columns), jnp.bfloat16)] * 3,
        input_output_aliases={6 + i: i for i in range(len(given))},
        compiler_params=pltpu.CompilerParams(vmem_limit_bytes=VMEM),
        cost_estimate=pl.CostEstimate(
            flops=96 * count * rows * size * size, bytes_accessed=22 * count * rows * size, transcendentals=0
        ),
        name="grads",
    )(place, *arrays, state, *given)


def swap(x, axis, offset):
    return lax.ppermute(x, axis, [(i, i ^ offset) for i in range(lax.axis_size(axis))])


def plane_sums(total):
    a, b = lax.axis_index("sa"), lax.axis_index("sb")
    kv = grad = jnp.zeros_like(total[0])
    chip = total
    for k in range(1, lax.axis_size("sb")):
        other = swap(total, "sb", k)
        chip = chip + other
        low = (b ^ k) < b
        kv = kv + jnp.where(low, other[0], 0.0)
        grad = grad + jnp.where(low, 0.0, other[1])
    for k in range(1, lax.axis_size("sa")):
        low = (a ^ k) < a
        other = swap(jnp.where(low, chip[1], chip[0]), "sa", k)
        kv = kv + jnp.where(low, other, 0.0)
        grad = grad + jnp.where(low, 0.0, other)
    return jnp.stack([kv, grad])


def shards(queries, key_rows, value_rows, out_grad, prefix_state, suffix_state):
    rows = queries.shape[0]
    head_count, size = prefix_state.shape[0], prefix_state.shape[1]
    devices = lax.axis_size("sa") * lax.axis_size("sb") * lax.axis_size("sc")
    factor = 1.0 / math.sqrt(size * rows * devices)
    c = lax.axis_index("sc")
    odd = c % 2
    arrays = (queries, key_rows, value_rows, out_grad)

    chunks, start = [], 0
    for heads, plane_first in CUTS:
        half = heads // 2
        own = start + odd * half
        his = start + (1 - odd) * half
        edge = jnp.stack(
            [lax.dynamic_slice_in_dim(s, own, half, 0) for s in (prefix_state, suffix_state)]
        )
        chunks.append((own, his, edge, plane_first))
        start += heads

    local = []
    for own, his, edge, plane_first in chunks:
        mine_his = local_terms(his, edge.shape[1], arrays, size)
        his_own = swap(mine_his, "sc", 1)
        mine_own = local_terms(own, edge.shape[1], arrays, size)
        local.append((mine_own, his_own))

    states = []
    for (own, his, edge, plane_first), (mine_own, his_own) in zip(chunks, local):
        pair = mine_own + his_own
        if plane_first:
            plane = plane_sums(pair)
            state = edge + plane
            for k in range(2, lax.axis_size("sc"), 2):
                low = (c ^ k) < c
                sent = plane + jnp.stack([jnp.where(low, 0.0, pair[0]), jnp.where(low, pair[1], 0.0)])
                state = state + swap(sent, "sc", k)
        else:
            total, state = pair, edge
            for k in range(2, lax.axis_size("sc"), 2):
                other = swap(pair, "sc", k)
                total = total + other
                low = (c ^ k) < c
                state = state + jnp.stack([jnp.where(low, other[0], 0.0), jnp.where(low, 0.0, other[1])])
            state = state + plane_sums(total)
        upper = odd == 1
        state_own = state + jnp.stack([jnp.where(upper, his_own[0], 0.0), jnp.where(upper, 0.0, his_own[1])])
        state_his = state + jnp.stack([jnp.where(upper, 0.0, mine_own[0]), jnp.where(upper, mine_own[1], 0.0)])
        states.append((state_own, swap(state_his, "sc", 1)))

    outs = None
    for (own, his, edge, plane_first), (state_own, state_other) in zip(chunks, states):
        outs = grads(own, arrays, state_own, outs, factor)
        outs = grads(his, arrays, state_other, outs, factor)
    return tuple(outs)


def solution(mesh):
    rows = P(AXES, None)
    return jax.shard_map(
        shards,
        mesh=mesh,
        in_specs=(rows, rows, rows, rows, P(), P()),
        out_specs=(rows, rows, rows),
        check_vma=False,
    )
```

```python
import functools
import math

import jax
import jax.numpy as jnp
from jax import lax
from jax.experimental import pallas as pl
from jax.experimental.pallas import tpu as pltpu
from jax.sharding import PartitionSpec as P

AXES = ("sa", "sb", "sc")
CHUNKS = ((6, False), (6, False), (4, True))
SPLIT = (2,)
ORDER = (
    "pair0",
    "inner1",
    "pair2",
    "inner0",
    "total0",
    "plane2",
    "pair1",
    "plane0",
    "found2",
    "inner2",
    "state2",
    "total1",
    "plane1",
    "found0",
    "state0",
    "own0",
    "found1",
    "finish2",
    "his0",
    "state1",
    "own2",
    "his2",
    "own1",
    "his1",
)
SWAPS = (2, 1)
COSTS = {'first': 100.0, 'load': 0.001, 'inner': 0.001, 'grads': 1000.0}
VMEM = 14 * 2**20
ROWS = 128
NN = (((1,), (0,)), ((), ()))
TN = (((0,), (0,)), ((), ()))


def cost(microseconds):
    return pl.CostEstimate(flops=int(microseconds * 1e6), bytes_accessed=0, transcendentals=0)


def split(x):
    high = x.astype(jnp.bfloat16)
    low = (x - high.astype(jnp.float32)).astype(jnp.bfloat16)
    return high, low


def wide(x):
    return jnp.concatenate(split(x), axis=1)


def fold(x):
    half = x.shape[1] // 2
    return x[:, :half] + x[:, half:]


def stacked(x):
    return jnp.concatenate([x, x], axis=0)


def dot(a, b):
    return lax.dot_general(a, b, NN, preferred_element_type=jnp.float32)


def outer(a, b):
    half = a.shape[1]
    full = fold(lax.dot_general(wide(a), wide(b), TN, preferred_element_type=jnp.float32))
    return full[:half] + full[half:]


IN_VMEM = pl.BlockSpec(memory_space=pltpu.VMEM)
IN_SMEM = pl.BlockSpec(memory_space=pltpu.SMEM)
ANYWHERE = pl.BlockSpec(memory_space=pl.ANY)


def in_vmem(x):
    return pltpu.with_memory_space_constraint(x, pltpu.VMEM)


def in_hbm(x):
    return pltpu.with_memory_space_constraint(x, pltpu.HBM)


def call(kernel, out_shape, out_specs, in_specs, microseconds, name, scratch_shapes=(), aliases=None):
    return pl.pallas_call(
        kernel,
        out_shape=out_shape,
        in_specs=in_specs,
        out_specs=out_specs,
        scratch_shapes=scratch_shapes,
        input_output_aliases=aliases or {},
        compiler_params=pltpu.CompilerParams(vmem_limit_bytes=VMEM),
        cost_estimate=cost(microseconds),
        name=name,
    )


def columns_at(head, size):
    if isinstance(head, int):
        return slice(head * size, (head + 1) * size)
    return pl.ds(pl.multiple_of(head * size, size), size)


def first_kernel(place_ref, q_ref, k_ref, v_ref, g_ref, out_ref, buffers, sems):
    count, size = out_ref.shape[1], out_ref.shape[-1]
    sources = (q_ref, k_ref, v_ref, g_ref)

    def copy(j, n):
        return pltpu.make_async_copy(
            sources[n].at[:, columns_at(place_ref[1, 0] + j, size)], buffers.at[j, n], sems.at[j, n]
        )

    for j in range(count):
        for n in range(4):
            copy(j, n).start()
    for j in range(count):
        for n in range(4):
            copy(j, n).wait()
        out_ref[0, j] = outer(buffers[j, 1], buffers[j, 2])
        out_ref[1, j] = outer(buffers[j, 3], buffers[j, 0])


def first_terms(places, count, arrays, size):
    rows = arrays[0].shape[0]
    return call(
        first_kernel,
        pltpu.VMEM((2, count, size, size), jnp.float32),
        IN_VMEM,
        [IN_SMEM] + [ANYWHERE] * 4,
        COSTS["first"],
        "first_terms",
        [pltpu.VMEM((count, 4, rows, size), jnp.float32), pltpu.SemaphoreType.DMA((count, 4))],
    )(places, *map(in_hbm, arrays))


def load_kernel(place_ref, q_ref, k_ref, v_ref, g_ref, prefix_ref, suffix_ref, *rest):
    chunks = (len(rest) - 5) // 3
    owns, others, edges = rest[:chunks], (None, *rest[chunks : 2 * chunks - 1]), rest[2 * chunks - 1 : 3 * chunks - 1]
    targets, sems, edge_sems = rest[-6:-2], rest[-2], rest[-1]
    sources = (q_ref, k_ref, v_ref, g_ref)
    size = owns[0].shape[-1]
    pieces = [(n, 0, owns[n]) for n in range(chunks)] + [(n, 1, others[n]) for n in range(chunks)]
    pieces = [pieces[0]] + [p for p in pieces[1:] if p[2] is not None] + [p for p in pieces if p[2] is None]

    def copies(n, side):
        first, count = place_ref[side, n], owns[n].shape[1]
        place = pl.ds(pl.multiple_of(first * size, size), count * size)
        return [
            pltpu.make_async_copy(sources[m].at[:, place], targets[m].at[:, place], sems.at[side, n, m])
            for m in range(4)
        ]

    def edge_copies(n):
        place = pl.ds(place_ref[0, n], owns[n].shape[1])
        return [
            pltpu.make_async_copy(ref.at[place], edges[n].at[m], edge_sems.at[n, m])
            for m, ref in enumerate((prefix_ref, suffix_ref))
        ]

    for n, side, _ in pieces:
        for copy in copies(n, side):
            copy.start()
    for n in range(chunks):
        for copy in edge_copies(n):
            copy.start()
    for n, side, out_ref in pieces:
        for copy in copies(n, side):
            copy.wait()
        if out_ref is None:
            continue

        @pl.loop(0, out_ref.shape[1])
        def _(j):
            place = columns_at(place_ref[side, n] + j, size)
            q, k, v, g = (ref[:, place] for ref in targets)
            out_ref[0, j] = outer(k, v)
            out_ref[1, j] = outer(g, q)

    for n in range(chunks):
        for copy in edge_copies(n):
            copy.wait()


def load_terms(places, halves, arrays, edges, size):
    kept = pltpu.VMEM(arrays[0].shape, arrays[0].dtype)
    terms = [pltpu.VMEM((2, half, size, size), jnp.float32) for half in halves]
    chunks = len(halves)
    results = call(
        load_kernel,
        terms + terms[1:] + terms + [kept] * 4,
        [IN_VMEM] * (3 * chunks + 3),
        [IN_SMEM] + [ANYWHERE] * 6,
        COSTS["load"],
        "load_terms",
        [pltpu.SemaphoreType.DMA((2, chunks, 4)), pltpu.SemaphoreType.DMA((chunks, 2))],
    )(places, *map(in_hbm, (*arrays, *edges)))
    return results[:chunks], results[chunks : 2 * chunks - 1], results[2 * chunks - 1 : 3 * chunks - 1], results[-4:]


def inner_grads(q, k, v, g):
    count, size = len(q), q[0].shape[1]
    row = lax.broadcasted_iota(jnp.int32, (size, size), 0)
    column = lax.broadcasted_iota(jnp.int32, (size, size), 1)
    lower, upper = row >= column, row <= column

    q_t, v_t, g_t = ([wide(x.T) for x in xs] for xs in (q, v, g))
    q, k, v, g = ([wide(x) for x in xs] for xs in (q, k, v, g))
    q_rows, k_rows, g_rows = ([stacked(x) for x in xs] for xs in (q, k, g))

    before_t, after, after_t = [None], [None], [None]
    for i in range(count - 1):
        j = count - 1 - i
        before_t.append(fold(dot(v_t[i], k_rows[i])))
        after.append(fold(dot(g_t[j], q_rows[j])))
        if i > 0:
            before_t[-1] = before_t[-1] + before_t[-2]
            after[-1] = after[-1] + after[-2]
        after_t.append(after[-1].T)
    after, after_t = after[::-1], after_t[::-1]

    def scores(a, b_t, mask):
        return wide(jnp.where(mask, fold(dot(a, stacked(b_t))), 0.0))

    def both(rows, state, weights, other_rows):
        if state is None:
            return fold(dot(weights, other_rows))
        left = jnp.concatenate([rows, weights], axis=1)
        right = jnp.concatenate([stacked(wide(state)), other_rows], axis=0)
        return fold(dot(left, right))

    for i in range(count):
        yield (
            both(g[i], before_t[i], scores(g[i], v_t[i], lower), k_rows[i]),
            both(v[i], after[i], scores(v[i], g_t[i], upper), q_rows[i]),
            both(k[i], after_t[i], scores(k[i], q_t[i], upper), g_rows[i]),
        )


def blocks_of(refs, place):
    size = ROWS
    return [[ref[i : i + size, place] for i in range(0, ref.shape[0], size)] for ref in refs]


def inner_kernel(first, q_ref, k_ref, v_ref, g_ref, tie_ref, out_ref):
    size = ROWS

    @pl.loop(0, out_ref.shape[2] // size)
    def _(j):
        for i, results in enumerate(inner_grads(*blocks_of((q_ref, k_ref, v_ref, g_ref), columns_at(first + j, size)))):
            for n, x in enumerate(results):
                out_ref[n, i * size : (i + 1) * size, columns_at(j, size)] = x


def inner_terms(first, count, arrays, size, tie):
    rows = arrays[0].shape[0]
    return call(
        functools.partial(inner_kernel, first),
        pltpu.VMEM((3, rows, count * size), jnp.float32),
        IN_VMEM,
        [IN_VMEM] * 4 + [ANYWHERE],
        COSTS["inner"] * count,
        "inner_terms",
    )(*map(in_vmem, arrays), tie)


def send_kernel(make, count, size, place_ref, outs, buffer, sems):
    def copy(j, n):
        return pltpu.make_async_copy(
            buffer.at[n, :, columns_at(j, size)], outs[n].at[:, columns_at(place_ref[0] + j, size)], sems.at[j, n]
        )

    @pl.loop(0, count)
    def _(j):
        make(j)
        for n in range(3):
            copy(j, n).start()

    for j in range(count):
        for n in range(3):
            copy(j, n).wait()


def state_kernel(factor, place_ref, k_ref, v_ref, g_ref, state_ref, inner_ref, *rest):
    outs, buffer, sems = rest[-5:-2], rest[-2], rest[-1]
    count, size = state_ref.shape[1], state_ref.shape[2]

    def make(j):
        place = columns_at(place_ref[0] + j, size)
        before, after = state_ref[0, j], state_ref[1, j]
        for n, (ref, state) in enumerate(((g_ref, before.T), (v_ref, after), (k_ref, after.T))):
            x = fold(dot(wide(ref[:, place]), stacked(wide(state))))
            x = x + inner_ref[n, :, columns_at(place_ref[1] + j, size)]
            buffer[n, :, columns_at(j, size)] = (factor * x).astype(buffer.dtype)

    send_kernel(make, count, size, place_ref, outs, buffer, sems)


def grads(place, arrays, state, inner, outs, factor):
    rows, columns = arrays[0].shape
    count, size = state.shape[1], state.shape[2]
    given = [] if outs is None else list(outs)
    operands = [*arrays[1:], state, inner]
    return call(
        functools.partial(state_kernel, factor),
        [jax.ShapeDtypeStruct((rows, columns), jnp.bfloat16)] * 3,
        [ANYWHERE] * 3,
        [IN_SMEM] + [IN_VMEM] * len(operands) + [ANYWHERE] * len(given),
        COSTS["grads"] * count,
        "state_grads",
        [pltpu.VMEM((3, rows, count * size), jnp.bfloat16), pltpu.SemaphoreType.DMA((count, 3))],
        {1 + len(operands) + n: n for n in range(len(given))},
    )(place, *map(in_vmem, operands), *given)


def swap(x, axis, offset, name):
    with jax.named_scope(name):
        return lax.ppermute(x, axis, [(i, i ^ offset) for i in range(lax.axis_size(axis))])


def pick(low, lower, upper):
    return jnp.where(low, lower, 0.0), jnp.where(low, 0.0, upper)


class Order:
    def __init__(self):
        self.last = None

    def then(self, x):
        if self.last is None:
            return x
        return lax.optimization_barrier((x, self.last))[0]

    def did(self, x):
        self.last = x
        return x


def shards(queries, key_rows, value_rows, out_grad, prefix_state, suffix_state):
    rows = queries.shape[0]
    heads, size = prefix_state.shape[:2]
    sizes = [lax.axis_size(axis) for axis in AXES]
    factor = 1.0 / math.sqrt(size * rows * math.prod(sizes))
    a, b, c = (lax.axis_index(axis) for axis in AXES)
    odd = c % 2
    upper = odd == 1
    arrays = (queries, key_rows, value_rows, out_grad)
    offsets = range(2, sizes[2], 2)
    chunks = range(len(CHUNKS))
    starts = [sum(count for count, _ in CHUNKS[:n]) for n in chunks]
    halves = [count // 2 for count, _ in CHUNKS]
    own = [start + odd * half for start, half in zip(starts, halves)]
    his = [start + (1 - odd) * half for start, half in zip(starts, halves)]
    pairs = {k: (c ^ k) < c for k in offsets}
    chips = {k: (b ^ k) < b for k in range(1, sizes[1])}
    faces = {k: (a ^ k) < a for k in range(1, sizes[0])}
    sides = jnp.stack([jnp.stack(own), jnp.stack(his)]).astype(jnp.int32)
    places = [
        [jnp.stack([first[n], first[n] - starts[n]]).astype(jnp.int32) for n in chunks] for first in (own, his)
    ]
    upper, pairs, chips, faces, sides, places = lax.optimization_barrier((upper, pairs, chips, faces, sides, places))
    order = Order()
    then, did = order.then, order.did

    first = did(first_terms(sides, halves[0], arrays, size))
    received = {0: swap(first, "sc", 1, "swap0")}
    mine, given, edge, arrays = load_terms(then(sides), halves, arrays, (prefix_state, suffix_state), size)
    did(mine[0])
    for n in SWAPS:
        received[n] = swap(given[n - 1], "sc", 1, f"swap{n}")
    total, found, waiting, extra, state, inners, results, outs = {}, {}, {}, {}, {}, {}, {}, [None]

    def both(low, lower, upper):
        return jnp.stack(pick(low, lower, upper))

    def pair(n):
        total[n] = did(mine[n] + then(received[n]))
        found[n] = edge[n]
        if not CHUNKS[n][1]:
            waiting[n] = [(pairs[k], swap(total[n], "sc", k, f"middle{n}")) for k in offsets]

    def total_(n):
        for low, other in waiting[n]:
            other = then(other)
            total[n] = total[n] + other
            found[n] = found[n] + both(low, other[0], other[1])
        did(total[n])

    def plane(n):
        x = then(total[n])
        waiting[n] = [(faces[k], swap(jnp.where(faces[k], x[1], x[0]), "sa", k, f"plane{n}")) for k in faces]

    def found_(n):
        x = 0.0
        for low, other in waiting[n]:
            other = then(other)
            x = x + both(low, other, other)
        extra[n] = did(x)
        waiting[n] = []
        for k in chips:
            down, up = pick(chips[k], total[n][1], total[n][0])
            if n in SPLIT:
                waiting[n].append([swap(x[0] + up, "sb", k, f"core{n}"), swap(x[1] + down, "sb", k, f"core{n}")])
            else:
                waiting[n].append([swap(x + jnp.stack([up, down]), "sb", k, f"core{n}")])

    def hand_back(n):
        theirs = then(received[n])
        state[n, 0] = state[n, 0] + found[n]
        state_his = did(state[n, 0] + jnp.stack(pick(upper, mine[n][1], mine[n][0])[::-1]))
        state[n, 0] = state[n, 0] + both(upper, theirs[0], theirs[1])
        state[n, 1] = swap(state_his, "sc", 1, f"back{n}")

    def state_(n):
        x = extra[n]
        for others in waiting[n]:
            others = [then(other) for other in others]
            x = x + (others[0] if len(others) == 1 else jnp.stack(others))
        state[n, 0] = x
        if not CHUNKS[n][1]:
            return hand_back(n)
        did(x)
        waiting[n] = []
        for k in offsets:
            down, up = pick(pairs[k], total[n][1], total[n][0])
            waiting[n].append(swap(x + jnp.stack([up, down]), "sc", k, f"middle{n}"))

    def finish(n):
        for other in waiting[n]:
            state[n, 0] = state[n, 0] + then(other)
        hand_back(n)

    def inner(n):
        inners[n] = did(inner_terms(starts[n], 2 * halves[n], arrays, size, order.last))

    def result(side, n):
        place = then(places[side][n])
        outs[0] = grads(place, arrays, then(state[n, side]), inners[n], outs[0], factor)
        did(outs[0])

    steps = {
        "pair": pair,
        "total": total_,
        "plane": plane,
        "found": found_,
        "state": state_,
        "finish": finish,
        "inner": inner,
        "own": functools.partial(result, 0),
        "his": functools.partial(result, 1),
    }
    for step in ORDER:
        steps[step[:-1]](int(step[-1]))
    return tuple(outs[0])


def solution(mesh):
    rows = P(AXES, None)
    return jax.shard_map(
        shards,
        mesh=mesh,
        in_specs=(rows, rows, rows, rows, P(), P()),
        out_specs=(rows, rows, rows),
        check_vma=False,
    )
```

```python
import functools
import math

import jax
import jax.numpy as jnp
from jax import lax
from jax.experimental import pallas as pl
from jax.experimental.pallas import tpu as pltpu
from jax.sharding import PartitionSpec as P

AXES = ("sa", "sb", "sc")
CHUNKS = ((6, False), (6, False), (4, True))
SPLIT = (0,)
ORDER = (
    "pair0",
    "mine1",
    "theirs1",
    "pair2",
    "plane2",
    "mine0",
    "found2",
    "pair1",
    "theirs0",
    "total0",
    "plane0",
    "mine2",
    "theirs2",
    "state2",
    "total1",
    "plane1",
    "found0",
    "state0",
    "own0",
    "found1",
    "finish2",
    "state1",
    "his0",
    "own2",
    "his2",
    "own1",
    "his1",
)
SWAPS = (2, 1)
COSTS = {'first': 100.0, 'load': 0.001, 'inner': 3000.0, 'grads': 1000.0}
VMEM = 14 * 2**20
ROWS = 128
NN = (((1,), (0,)), ((), ()))
TN = (((0,), (0,)), ((), ()))


def cost(microseconds):
    return pl.CostEstimate(flops=int(microseconds * 1e6), bytes_accessed=0, transcendentals=0)


def split(x):
    high = x.astype(jnp.bfloat16)
    low = (x - high.astype(jnp.float32)).astype(jnp.bfloat16)
    return high, low


def wide(x):
    return jnp.concatenate(split(x), axis=1)


def fold(x):
    half = x.shape[1] // 2
    return x[:, :half] + x[:, half:]


def stacked(x):
    return jnp.concatenate([x, x], axis=0)


def dot(a, b):
    return lax.dot_general(a, b, NN, preferred_element_type=jnp.float32)


def outer(a, b):
    half = a.shape[1]
    full = fold(lax.dot_general(wide(a), wide(b), TN, preferred_element_type=jnp.float32))
    return full[:half] + full[half:]


IN_VMEM = pl.BlockSpec(memory_space=pltpu.VMEM)
IN_SMEM = pl.BlockSpec(memory_space=pltpu.SMEM)
ANYWHERE = pl.BlockSpec(memory_space=pl.ANY)


def in_vmem(x):
    return pltpu.with_memory_space_constraint(x, pltpu.VMEM)


def in_hbm(x):
    return pltpu.with_memory_space_constraint(x, pltpu.HBM)


def call(kernel, out_shape, out_specs, in_specs, microseconds, name, scratch_shapes=(), aliases=None):
    return pl.pallas_call(
        kernel,
        out_shape=out_shape,
        in_specs=in_specs,
        out_specs=out_specs,
        scratch_shapes=scratch_shapes,
        input_output_aliases=aliases or {},
        compiler_params=pltpu.CompilerParams(vmem_limit_bytes=VMEM),
        cost_estimate=cost(microseconds),
        name=name,
    )


def columns_at(head, size):
    if isinstance(head, int):
        return slice(head * size, (head + 1) * size)
    return pl.ds(pl.multiple_of(head * size, size), size)


def first_kernel(place_ref, q_ref, k_ref, v_ref, g_ref, out_ref, buffers, sems):
    count, size = out_ref.shape[1], out_ref.shape[-1]
    sources = (q_ref, k_ref, v_ref, g_ref)

    def copy(j, n):
        return pltpu.make_async_copy(
            sources[n].at[:, columns_at(place_ref[1, 0] + j, size)], buffers.at[j, n], sems.at[j, n]
        )

    for j in range(count):
        for n in range(4):
            copy(j, n).start()
    for j in range(count):
        for n in range(4):
            copy(j, n).wait()
        out_ref[0, j] = outer(buffers[j, 1], buffers[j, 2])
        out_ref[1, j] = outer(buffers[j, 3], buffers[j, 0])


def first_terms(places, count, arrays, size):
    rows = arrays[0].shape[0]
    return call(
        first_kernel,
        pltpu.VMEM((2, count, size, size), jnp.float32),
        IN_VMEM,
        [IN_SMEM] + [ANYWHERE] * 4,
        COSTS["first"],
        "first_terms",
        [pltpu.VMEM((count, 4, rows, size), jnp.float32), pltpu.SemaphoreType.DMA((count, 4))],
    )(places, *map(in_hbm, arrays))


def load_kernel(place_ref, q_ref, k_ref, v_ref, g_ref, prefix_ref, suffix_ref, *rest):
    chunks = (len(rest) - 5) // 3
    owns, others, edges = rest[:chunks], (None, *rest[chunks : 2 * chunks - 1]), rest[2 * chunks - 1 : 3 * chunks - 1]
    targets, sems, edge_sems = rest[-6:-2], rest[-2], rest[-1]
    sources = (q_ref, k_ref, v_ref, g_ref)
    size = owns[0].shape[-1]
    pieces = [(n, 0, owns[n]) for n in range(chunks)] + [(n, 1, others[n]) for n in range(chunks)]
    pieces = [pieces[0]] + [p for p in pieces[1:] if p[2] is not None] + [p for p in pieces if p[2] is None]

    def copies(n, side):
        first, count = place_ref[side, n], owns[n].shape[1]
        place = pl.ds(pl.multiple_of(first * size, size), count * size)
        return [
            pltpu.make_async_copy(sources[m].at[:, place], targets[m].at[:, place], sems.at[side, n, m])
            for m in range(4)
        ]

    def edge_copies(n):
        place = pl.ds(place_ref[0, n], owns[n].shape[1])
        return [
            pltpu.make_async_copy(ref.at[place], edges[n].at[m], edge_sems.at[n, m])
            for m, ref in enumerate((prefix_ref, suffix_ref))
        ]

    for n, side, _ in pieces:
        for copy in copies(n, side):
            copy.start()
    for n in range(chunks):
        for copy in edge_copies(n):
            copy.start()
    for n, side, out_ref in pieces:
        for copy in copies(n, side):
            copy.wait()
        if out_ref is None:
            continue

        @pl.loop(0, out_ref.shape[1])
        def _(j):
            place = columns_at(place_ref[side, n] + j, size)
            q, k, v, g = (ref[:, place] for ref in targets)
            out_ref[0, j] = outer(k, v)
            out_ref[1, j] = outer(g, q)

    for n in range(chunks):
        for copy in edge_copies(n):
            copy.wait()


def load_terms(places, halves, arrays, edges, size):
    kept = pltpu.VMEM(arrays[0].shape, arrays[0].dtype)
    terms = [pltpu.VMEM((2, half, size, size), jnp.float32) for half in halves]
    chunks = len(halves)
    results = call(
        load_kernel,
        terms + terms[1:] + terms + [kept] * 4,
        [IN_VMEM] * (3 * chunks + 3),
        [IN_SMEM] + [ANYWHERE] * 6,
        COSTS["load"],
        "load_terms",
        [pltpu.SemaphoreType.DMA((2, chunks, 4)), pltpu.SemaphoreType.DMA((chunks, 2))],
    )(places, *map(in_hbm, (*arrays, *edges)))
    return results[:chunks], results[chunks : 2 * chunks - 1], results[2 * chunks - 1 : 3 * chunks - 1], results[-4:]


def inner_grads(q, k, v, g):
    count, size = len(q), q[0].shape[1]
    row = lax.broadcasted_iota(jnp.int32, (size, size), 0)
    column = lax.broadcasted_iota(jnp.int32, (size, size), 1)
    lower, upper = row >= column, row <= column

    q_t, v_t, g_t = ([wide(x.T) for x in xs] for xs in (q, v, g))
    q, k, v, g = ([wide(x) for x in xs] for xs in (q, k, v, g))
    q_rows, k_rows, g_rows = ([stacked(x) for x in xs] for xs in (q, k, g))

    before_t, after, after_t = [None], [None], [None]
    for i in range(count - 1):
        j = count - 1 - i
        before_t.append(fold(dot(v_t[i], k_rows[i])))
        after.append(fold(dot(g_t[j], q_rows[j])))
        if i > 0:
            before_t[-1] = before_t[-1] + before_t[-2]
            after[-1] = after[-1] + after[-2]
        after_t.append(after[-1].T)
    after, after_t = after[::-1], after_t[::-1]

    def scores(a, b_t, mask):
        return wide(jnp.where(mask, fold(dot(a, stacked(b_t))), 0.0))

    def both(rows, state, weights, other_rows):
        if state is None:
            return fold(dot(weights, other_rows))
        left = jnp.concatenate([rows, weights], axis=1)
        right = jnp.concatenate([stacked(wide(state)), other_rows], axis=0)
        return fold(dot(left, right))

    for i in range(count):
        yield (
            both(g[i], before_t[i], scores(g[i], v_t[i], lower), k_rows[i]),
            both(v[i], after[i], scores(v[i], g_t[i], upper), q_rows[i]),
            both(k[i], after_t[i], scores(k[i], q_t[i], upper), g_rows[i]),
        )


def blocks_of(refs, place):
    size = ROWS
    return [[ref[i : i + size, place] for i in range(0, ref.shape[0], size)] for ref in refs]


def inner_kernel(place_ref, q_ref, k_ref, v_ref, g_ref, out_ref):
    size = ROWS

    @pl.loop(0, out_ref.shape[2] // size)
    def _(j):
        for i, results in enumerate(inner_grads(*blocks_of((q_ref, k_ref, v_ref, g_ref), columns_at(place_ref[0] + j, size)))):
            for n, x in enumerate(results):
                out_ref[n, i * size : (i + 1) * size, columns_at(j, size)] = x


def inner_terms(place, count, arrays, size):
    rows = arrays[0].shape[0]
    return call(
        inner_kernel,
        pltpu.VMEM((3, rows, count * size), jnp.float32),
        IN_VMEM,
        [IN_SMEM] + [IN_VMEM] * 4,
        COSTS["inner"] * count,
        "inner_terms",
    )(place, *map(in_vmem, arrays))


def send_kernel(make, count, size, place_ref, outs, buffer, sems):
    def copy(j, n):
        return pltpu.make_async_copy(
            buffer.at[n, :, columns_at(j, size)], outs[n].at[:, columns_at(place_ref[0] + j, size)], sems.at[j, n]
        )

    @pl.loop(0, count)
    def _(j):
        make(j)
        for n in range(3):
            copy(j, n).start()

    for j in range(count):
        for n in range(3):
            copy(j, n).wait()


def state_kernel(factor, place_ref, k_ref, v_ref, g_ref, state_ref, inner_ref, *rest):
    outs, buffer, sems = rest[-5:-2], rest[-2], rest[-1]
    count, size = state_ref.shape[1], state_ref.shape[2]

    def make(j):
        place = columns_at(place_ref[0] + j, size)
        before, after = state_ref[0, j], state_ref[1, j]
        for n, (ref, state) in enumerate(((g_ref, before.T), (v_ref, after), (k_ref, after.T))):
            x = fold(dot(wide(ref[:, place]), stacked(wide(state))))
            x = x + inner_ref[n, :, columns_at(j, size)]
            buffer[n, :, columns_at(j, size)] = (factor * x).astype(buffer.dtype)

    send_kernel(make, count, size, place_ref, outs, buffer, sems)


def grads(place, arrays, state, inner, outs, factor):
    rows, columns = arrays[0].shape
    count, size = state.shape[1], state.shape[2]
    given = [] if outs is None else list(outs)
    operands = [*arrays[1:], state, inner]
    return call(
        functools.partial(state_kernel, factor),
        [jax.ShapeDtypeStruct((rows, columns), jnp.bfloat16)] * 3,
        [ANYWHERE] * 3,
        [IN_SMEM] + [IN_VMEM] * len(operands) + [ANYWHERE] * len(given),
        COSTS["grads"] * count,
        "state_grads",
        [pltpu.VMEM((3, rows, count * size), jnp.bfloat16), pltpu.SemaphoreType.DMA((count, 3))],
        {1 + len(operands) + n: n for n in range(len(given))},
    )(place, *map(in_vmem, operands), *given)


def swap(x, axis, offset, name):
    with jax.named_scope(name):
        return lax.ppermute(x, axis, [(i, i ^ offset) for i in range(lax.axis_size(axis))])


def pick(low, lower, upper):
    return jnp.where(low, lower, 0.0), jnp.where(low, 0.0, upper)


class Order:
    def __init__(self):
        self.last = None

    def then(self, x):
        if self.last is None:
            return x
        return lax.optimization_barrier((x, self.last))[0]

    def did(self, x):
        self.last = x
        return x


def shards(queries, key_rows, value_rows, out_grad, prefix_state, suffix_state):
    rows = queries.shape[0]
    heads, size = prefix_state.shape[:2]
    sizes = [lax.axis_size(axis) for axis in AXES]
    factor = 1.0 / math.sqrt(size * rows * math.prod(sizes))
    a, b, c = (lax.axis_index(axis) for axis in AXES)
    odd = c % 2
    upper = odd == 1
    arrays = (queries, key_rows, value_rows, out_grad)
    offsets = range(2, sizes[2], 2)
    chunks = range(len(CHUNKS))
    starts = [sum(count for count, _ in CHUNKS[:n]) for n in chunks]
    halves = [count // 2 for count, _ in CHUNKS]
    own = [start + odd * half for start, half in zip(starts, halves)]
    his = [start + (1 - odd) * half for start, half in zip(starts, halves)]
    pairs = {k: (c ^ k) < c for k in offsets}
    chips = {k: (b ^ k) < b for k in range(1, sizes[1])}
    faces = {k: (a ^ k) < a for k in range(1, sizes[0])}
    sides = jnp.stack([jnp.stack(own), jnp.stack(his)]).astype(jnp.int32)
    places = [
        [first[n].astype(jnp.int32).reshape(1) for n in chunks] for first in (own, his)
    ]
    upper, pairs, chips, faces, sides, places = lax.optimization_barrier((upper, pairs, chips, faces, sides, places))
    order = Order()
    then, did = order.then, order.did

    first = did(first_terms(sides, halves[0], arrays, size))
    received = {0: swap(first, "sc", 1, "swap0")}
    mine, given, edge, arrays = load_terms(then(sides), halves, arrays, (prefix_state, suffix_state), size)
    did(mine[0])
    for n in SWAPS:
        received[n] = swap(given[n - 1], "sc", 1, f"swap{n}")
    total, found, waiting, extra, state, inners, results, outs = {}, {}, {}, {}, {}, {}, {}, [None]

    def both(low, lower, upper):
        return jnp.stack(pick(low, lower, upper))

    def pair(n):
        total[n] = did(mine[n] + then(received[n]))
        found[n] = edge[n]
        if not CHUNKS[n][1]:
            waiting[n] = [(pairs[k], swap(total[n], "sc", k, f"middle{n}")) for k in offsets]

    def total_(n):
        for low, other in waiting[n]:
            other = then(other)
            total[n] = total[n] + other
            found[n] = found[n] + both(low, other[0], other[1])
        did(total[n])

    def plane(n):
        x = then(total[n])
        waiting[n] = [(faces[k], swap(jnp.where(faces[k], x[1], x[0]), "sa", k, f"plane{n}")) for k in faces]

    def found_(n):
        x = 0.0
        for low, other in waiting[n]:
            other = then(other)
            x = x + both(low, other, other)
        extra[n] = did(x)
        waiting[n] = []
        for k in chips:
            down, up = pick(chips[k], total[n][1], total[n][0])
            if n in SPLIT:
                waiting[n].append([swap(x[0] + up, "sb", k, f"core{n}"), swap(x[1] + down, "sb", k, f"core{n}")])
            else:
                waiting[n].append([swap(x + jnp.stack([up, down]), "sb", k, f"core{n}")])

    def hand_back(n):
        theirs = then(received[n])
        state[n, 0] = state[n, 0] + found[n]
        state_his = did(state[n, 0] + jnp.stack(pick(upper, mine[n][1], mine[n][0])[::-1]))
        state[n, 0] = state[n, 0] + both(upper, theirs[0], theirs[1])
        state[n, 1] = swap(state_his, "sc", 1, f"back{n}")

    def state_(n):
        x = extra[n]
        for others in waiting[n]:
            others = [then(other) for other in others]
            x = x + (others[0] if len(others) == 1 else jnp.stack(others))
        state[n, 0] = x
        if not CHUNKS[n][1]:
            return hand_back(n)
        did(x)
        waiting[n] = []
        for k in offsets:
            down, up = pick(pairs[k], total[n][1], total[n][0])
            waiting[n].append(swap(x + jnp.stack([up, down]), "sc", k, f"middle{n}"))

    def finish(n):
        for other in waiting[n]:
            state[n, 0] = state[n, 0] + then(other)
        hand_back(n)

    def inner(side, n):
        inners[n, side] = did(inner_terms(then(places[side][n]), halves[n], arrays, size))

    def result(side, n):
        place = then(places[side][n])
        outs[0] = grads(place, arrays, then(state[n, side]), inners[n, side], outs[0], factor)
        did(outs[0])

    steps = {
        "pair": pair,
        "total": total_,
        "plane": plane,
        "found": found_,
        "state": state_,
        "finish": finish,
        "mine": functools.partial(inner, 0),
        "theirs": functools.partial(inner, 1),
        "own": functools.partial(result, 0),
        "his": functools.partial(result, 1),
    }
    for step in ORDER:
        steps[step[:-1]](int(step[-1]))
    return tuple(outs[0])


def solution(mesh):
    rows = P(AXES, None)
    return jax.shard_map(
        shards,
        mesh=mesh,
        in_specs=(rows, rows, rows, rows, P(), P()),
        out_specs=(rows, rows, rows),
        check_vma=False,
    )
```
